256 devices in a mesh: rows: 16 (over z, y_lo), cols: 16 (over x, y_hi, core).
Axes of the slice: x: 4, y: 4 (y_hi: 2, y_lo: 2; y = y_hi * 2 + y_lo), z: 8, core: 2. Of those that a mesh axis runs over, the one named last changes fastest.
Arguments:
- operator: float32 [4096, 4096], P('rows', 'cols'), may hold values from -6 to 6
- basis: float32 [4096, 4096], P('rows', 'cols'), may hold values from -0.09375 to 0.09375
- split_rank: int32 [1], replicated, may hold values from 1024 to 3072
Outputs:
- projected: float32 [4096, 4096], P('rows', 'cols')
The draws below stay inside these ranges and needn't reach their ends.
All inputs are finite; a program needn't handle non-finite values.
Results may differ from the reference program's by a relative error of at most 0.00011.
Values sent between devices are 32-bit elements; how exact they have to be, the bound alone decides.
No kernel may reach another device: no remote copies, remote signals or barrier semaphores. Data moves between devices by JAX's collectives and lax.ppermute only.
A program may use at most 64 MiB of HBM per device.

```python
import jax
import jax.numpy as jnp
from jax import lax

N = 4096


def block_scale(key, shape, split, smallest, top_value):
    gain = 1.0
    for dim, blocks in split:
        steps = jax.random.uniform(jax.random.fold_in(jax.random.fold_in(key, 6), dim), (blocks,), jnp.float32, smallest / len(split), top_value / len(split))
        gain = gain * jnp.repeat(jnp.exp(steps), shape[dim] // blocks).reshape((-1,) + (1,) * (len(shape) - 1 - dim))
    return gain


def noise(own_key, dims, deviation, reach, pieces=(), kind=jnp.bfloat16):
    gain = block_scale(own_key, dims, pieces, -0.22, 0.18) if pieces else 1.0
    result = jax.random.normal(own_key, dims, jnp.float32) * deviation * gain
    return jnp.minimum(jnp.maximum(result, -reach), reach).astype(kind)


def setup_inputs(seed: int = 0) -> dict:
    splits = jax.random.split(jax.random.key(seed), 4)
    return {
        "operator": noise(splits[0], (N, N), 1.0, 6.0, ((0, 16), (1, 16)), jnp.float32),
        "basis": noise(splits[1], (N, N), N ** -0.5, 0.09375, ((0, 16), (1, 16)), jnp.float32),
        "split_rank": jax.random.randint(splits[2], (1,), N // 4, 3 * N // 4 + 1).astype(jnp.int32),
    }


def reference(operator, basis, split_rank):
    image = jnp.dot(operator, basis, precision=lax.Precision.HIGHEST, preferred_element_type=jnp.float32)
    forward = jnp.dot(basis.T, image, precision=lax.Precision.HIGHEST, preferred_element_type=jnp.float32)
    backward = jnp.dot(image.T, basis, precision=lax.Precision.HIGHEST, preferred_element_type=jnp.float32)
    symmetric = 0.5 * (forward + backward)
    index = jnp.arange(N, dtype=jnp.int32)
    first = index < split_rank[0]
    keep = first[:, None] == first[None, :]
    return jnp.where(keep, symmetric, jnp.float32(0.0))
```

```python
import jax
import jax.numpy as jnp
from jax import lax
from jax.experimental import pallas as pl
from jax.experimental.pallas import tpu as pltpu
from jax.sharding import PartitionSpec as P

Z, X = 8, 4
AXES = ("rows", "cols")
T = 256
H = T // 2
VMEM_LIMIT = 48 * 1024 * 1024


def _place(d):
    r, c = divmod(d, 16)
    return r // 2, r % 2, c // 4, (c // 2) % 2, c % 2


def _device(z, yl, x, yh, core):
    return (z % Z * 2 + yl) * 16 + (x % X) * 4 + yh * 2 + core


def _send(a, to):
    return lax.ppermute(a, AXES, [(d, _device(*to(*_place(d)))) for d in range(256)])


def swap(a):
    return _send(a, lambda z, yl, x, yh, core: (z, core, x, yh, yl))


def shift_z(a, k):
    return _send(a, lambda z, yl, x, yh, core: (z + k, yl, x, yh, core))


def shift_x(a, k):
    return _send(a, lambda z, yl, x, yh, core: (z, yl, x + k, yh, core))


def flip_yh(a):
    return _send(a, lambda z, yl, x, yh, core: (z, yl, x, 1 - yh, core))


def flip_yl(a):
    return _send(a, lambda z, yl, x, yh, core: (z, 1 - yl, x, yh, core))


def flip_core(a):
    return _send(a, lambda z, yl, x, yh, core: (z, yl, x, yh, 1 - core))


PANEL = [(dx, dy) for dy in (0, 1) for dx in (0, -1, 1, 2)]
RING = (0, -1, 1, -2, 2, -3, 3, 4)


def gather_xyh(a):
    other = flip_yh(a)
    blocks = []
    for b in (a, other):
        blocks += [b, shift_x(b, 1), shift_x(b, -1), shift_x(b, 2)]
    return blocks


def gather_z(a):
    right, left = [a[:H], a[H:]], [a[:H], a[H:]]
    blocks = [right]
    for _ in range(3):
        right = [shift_z(h, 1) for h in right]
        left = [shift_z(h, -1) for h in left]
        blocks += [right, left]
    blocks.append([shift_z(right[0], 1), shift_z(left[1], -1)])
    return blocks


def split(a):
    hi = a.astype(jnp.bfloat16)
    return hi, (a - hi.astype(jnp.float32)).astype(jnp.bfloat16)


def panel_place(place, dx, dy):
    return lax.rem(place[2] + dx + X, X) * 2 + lax.rem(place[3] + dy, 2)


def dot3(ah, al, bh, bl, dims):
    def dot(a, b):
        return lax.dot_general(a, b, (dims, ((), ())), preferred_element_type=jnp.float32)
    return dot(al, bh) + dot(ah, bl) + dot(ah, bh)


def image_kernel(place, *refs):
    a, own, other = refs[:8], refs[8:24], refs[24:40]
    keep, send, ah, al, bh, bl = refs[40:]
    z, yl, core = place[0], place[1], place[4]
    for (dx, dy), ref in zip(PANEL, a):
        at = pl.multiple_of(panel_place(place, dx, dy) * T, T)
        ah[:, pl.ds(at, T)], al[:, pl.ds(at, T)] = split(ref[...])
    for q, blocks in ((core, own), (1 - core, other)):
        for i, dz in enumerate(RING):
            for h in range(2):
                at = pl.multiple_of(lax.rem(z + dz + Z, Z) * T + h * H, H)
                bh[q, pl.ds(at, H)], bl[q, pl.ds(at, H)] = split(blocks[2 * i + h][...])
    for q, out in ((1 - yl, send), (yl, keep)):
        out[...] = dot3(ah[...], al[...], bh[q], bl[q], ((1,), (0,)))


def project_kernel(place, *refs):
    pb, pi = refs[:8], refs[8:16]
    b_same, b_flip, i_same, i_flip = refs[16:20]
    own, other, lh, ll, rh, rl = refs[20:]
    z, yl, core = place[0], place[1], place[4]
    for half, blocks in enumerate((pb, pi)):
        for (dx, dy), ref in zip(PANEL, blocks):
            at = panel_place(place, dx, dy)
            rows = pl.ds(half * T, T)
            lh[at, rows], ll[at, rows] = split(ref[...])
    for half, (same, flip) in enumerate(((i_same, i_flip), (b_same, b_flip))):
        rows = pl.ds(half * T, T)
        rh[yl, rows], rl[yl, rows] = split(same[...])
        rh[1 - yl, rows], rl[1 - yl, rows] = split(flip[...])

    def step(d, _):
        at = lax.rem(z + d, Z)
        for q, out in ((core, own), (1 - core, other)):
            out[d] = dot3(lh[at], ll[at], rh[q], rl[q], ((0,), (0,)))
        return 0

    lax.fori_loop(0, Z, step, 0)


def vmem(n):
    return [pl.BlockSpec(memory_space=pltpu.VMEM)] * n


def kernel(body, place, args, out_shape, scratch):
    return pl.pallas_call(
        body,
        out_shape=out_shape,
        in_specs=[pl.BlockSpec(memory_space=pltpu.SMEM)] + vmem(len(args)),
        out_specs=[pl.BlockSpec(memory_space=pltpu.VMEM)] * len(out_shape),
        scratch_shapes=scratch,
        compiler_params=pltpu.CompilerParams(vmem_limit_bytes=VMEM_LIMIT),
    )(place, *args)


def local(operator, basis, split_rank):
    row, col = lax.axis_index("rows"), lax.axis_index("cols")
    place = jnp.stack([row // 2, row % 2, col // 4, (col // 2) % 2, col % 2]).astype(jnp.int32)
    f32, bf16 = jnp.float32, jnp.bfloat16
    block = jax.ShapeDtypeStruct((T, T), f32)

    a_panel = gather_xyh(swap(operator))
    halves = [h for pair in gather_z(basis) for h in pair]
    others = [flip_core(h) for h in halves]
    b_swapped = swap(basis)
    b_panel = gather_xyh(b_swapped)
    b_flip = flip_yl(b_swapped)

    keep, send = kernel(
        image_kernel, place, a_panel + halves + others, [block, block],
        [pltpu.VMEM((T, Z * T), bf16)] * 2 + [pltpu.VMEM((2, Z * T, T), bf16)] * 2,
    )
    image = keep + flip_yl(send)
    i_flip = flip_yl(image)
    i_panel = gather_xyh(image)
    stack = jax.ShapeDtypeStruct((Z, T, T), f32)
    own, other = kernel(
        project_kernel, place, b_panel + i_panel + [b_swapped, b_flip, image, i_flip], [stack, stack],
        [pltpu.VMEM((Z, 2 * T, T), bf16)] * 2 + [pltpu.VMEM((2, 2 * T, T), bf16)] * 2,
    )
    part = {}
    for d in (4, 3, 5, 2, 6, 1, 7, 0):
        whole = own[d] + flip_core(other[d])
        part[d] = whole[:H], whole[H:]
    right = [part[4][0], part[3][1]]
    left = [part[5][0], part[4][1]]
    right[0], left[1] = shift_z(right[0], 1) + part[3][0], shift_z(left[1], -1) + part[5][1]
    for k in (2, 1, 0):
        right = [shift_z(r, 1) + part[k][h] for h, r in enumerate(right)]
        left = [shift_z(l, -1) + (part[Z - k][h] if k else 0.0) for h, l in enumerate(left)]
    symmetric = 0.5 * jnp.concatenate([right[h] + left[h] for h in range(2)])
    row_index = row * T + jnp.arange(T, dtype=jnp.int32)
    col_index = col * T + jnp.arange(T, dtype=jnp.int32)
    limit = split_rank[0]
    same = (row_index < limit)[:, None] == (col_index < limit)[None, :]
    return jnp.where(same, symmetric, jnp.float32(0.0))


def solution(mesh):
    in_specs = (P("rows", "cols"), P("rows", "cols"), P())
    return jax.shard_map(local, mesh=mesh, in_specs=in_specs, out_specs=P("rows", "cols"), check_vma=False)
```

```python
import jax
import jax.numpy as jnp
from jax import lax
from jax.experimental import pallas as pl
from jax.experimental.pallas import tpu as pltpu
from jax.sharding import Mesh, PartitionSpec as P

Z, X = 8, 4
AXES = ("z", "yl", "x", "yh", "core")
ROWS, COLS = AXES[:2], AXES[2:]
T = 256
H = T // 2
VMEM_LIMIT = 24 * 1024 * 1024
CHUNKS = 2


def _place(d):
    r, c = divmod(d, 16)
    return r // 2, r % 2, c // 4, (c // 2) % 2, c % 2


def _device(z, yl, x, yh, core):
    return (z % Z * 2 + yl) * 16 + (x % X) * 4 + yh * 2 + core


def _send(a, to):
    return lax.ppermute(a, AXES, [(d, _device(*to(*_place(d)))) for d in range(256)])


def swap(a):
    return _send(a, lambda z, yl, x, yh, core: (z, core, x, yh, yl))


def shift_z(a, k):
    return _send(a, lambda z, yl, x, yh, core: (z + k, yl, x, yh, core))


def shift_x(a, k):
    return _send(a, lambda z, yl, x, yh, core: (z, yl, x + k, yh, core))


def flip_yh(a):
    return _send(a, lambda z, yl, x, yh, core: (z, yl, x, 1 - yh, core))


def shift_y(a, k):
    def to(z, yl, x, yh, core):
        y = (2 * yh + yl + k) % 4
        return z, y % 2, x, y // 2, core
    return _send(a, to)


def flip_pair(a):
    return _send(a, lambda z, yl, x, yh, core: (z // 2 * 2 + yh, yl, x, z % 2, core))


def flip_yl(a):
    return _send(a, lambda z, yl, x, yh, core: (z, 1 - yl, x, yh, core))


def flip_core(a):
    return _send(a, lambda z, yl, x, yh, core: (z, yl, x, yh, 1 - core))


FOUR = (0, -1, 1, 2)
PANEL = [(dx, dy) for dy in (0, 1) for dx in FOUR]
RING = (0, -1, 1, -2, 2, -3, 3, 4)


def after(a, *others):
    return lax.optimization_barrier((a, others))[0]


def gather_x(a):
    return [a, shift_x(a, 1), shift_x(a, -1), shift_x(a, 2)]


def gather_y(a):
    return [a, shift_y(a, 1), shift_y(a, -1), shift_y(a, 2)]


def split(a):
    hi = a.astype(jnp.bfloat16)
    return hi, (a - hi.astype(jnp.float32)).astype(jnp.bfloat16)


def panel_place(place, dx, dy):
    return lax.rem(place[2] + dx + X, X) * 2 + lax.rem(place[3] + dy, 2)


def dot3(ah, al, bh, bl):
    def dot(a, b):
        return jnp.dot(a, b, preferred_element_type=jnp.float32)
    return dot(al, bh) + dot(ah, bl) + dot(ah, bh)


def fetch(refs, stage, sems):
    copies = [pltpu.make_async_copy(ref, stage.at[i], sems.at[i]) for i, ref in enumerate(refs)]
    for copy in copies:
        copy.start()
    return copies


def image_kernel(place, *refs):
    a, own, other = refs[:8], refs[8:17], refs[17:26]
    keep, send, stage, ends, sems, end_sems, ah, al, bh, bl = refs[26:]
    z, yl, core = place[0], place[1], place[4]
    copies = fetch(a + own[:7] + other[:7], stage, sems)
    end_copies = fetch(own[7:] + other[7:], ends, end_sems)
    for i, (dx, dy) in enumerate(PANEL):
        copies[i].wait()
        at = pl.multiple_of(panel_place(place, dx, dy) * T, T)
        ah[:, pl.ds(at, T)], al[:, pl.ds(at, T)] = split(stage[i])
    for k, q in enumerate((core, 1 - core)):
        for i, dz in enumerate(RING[:7]):
            slot = 8 + 7 * k + i
            copies[slot].wait()
            at = pl.multiple_of(lax.rem(z + dz + Z, Z) * T, T)
            bh[q, pl.ds(at, T)], bl[q, pl.ds(at, T)] = split(stage[slot])
        for h in range(2):
            end_copies[2 * k + h].wait()
            at = pl.multiple_of(lax.rem(z + RING[7], Z) * T + h * H, H)
            bh[q, pl.ds(at, H)], bl[q, pl.ds(at, H)] = split(ends[2 * k + h])
    for q, out in ((1 - yl, send), (yl, keep)):
        out[...] = dot3(ah[...], al[...], bh[q], bl[q])


def prepare_kernel(place, *refs):
    bx, by = refs[:4], refs[4:8]
    rh, rl, lh, ll, stage, sems = refs[8:]
    x, y = place[2], 2 * place[3] + place[1]
    copies = fetch(bx + by, stage, sems)
    for i, d in enumerate(FOUR):
        copies[i].wait()
        at = lax.rem(x + d + 4, 4)
        rh[at], rl[at] = split(stage[i])
    for i, d in enumerate(FOUR):
        copies[4 + i].wait()
        at = lax.rem(y + d + 4, 4)
        lh[at], ll[at] = split(stage[4 + i].T)


FIRST, REST = (4, 3, 5), (2, 6, 1, 7, 0)


def first_kernel(place, *refs):
    ix, iy, basis = refs[:4], refs[4:8], refs[8:12]
    out, image = refs[12:12 + 2 * len(FIRST)], refs[12 + 2 * len(FIRST):]
    rh, rl, lh, ll = image
    x, y = place[2], 2 * place[3] + place[1]
    for ref, d in zip(ix, FOUR):
        at = lax.rem(x + d + 4, 4)
        rh[at], rl[at] = split(ref[...])
    for ref, d in zip(iy, FOUR):
        at = lax.rem(y + d + 4, 4)
        lh[at], ll[at] = split(ref[...].T)
    products(place, basis, image, out, FIRST)


def rest_kernel(place, *refs):
    products(place, refs[:4], refs[4:8], refs[8:], REST)


def products(place, basis, image, out, where):
    brh, brl, blh, bll = basis
    irh, irl, ilh, ill = image
    z, core = place[0], place[4]
    for q, refs in ((1 - core, out[len(where):]), (core, out[:len(where)])):
        for d, ref in zip(where, refs):
            at = lax.rem(z + d, Z)
            r, l = at // 2, 2 * lax.rem(at, 2) + q
            ref[...] = (dot3(ilh[l], ill[l], brh[r], brl[r]) + dot3(blh[l], bll[l], irh[r], irl[r]))


VMEM, HBM = pl.BlockSpec(memory_space=pltpu.VMEM), pl.BlockSpec(memory_space=pltpu.HBM)


def kernel(body, place, far, near, out_shape, scratch=(), flops=0):
    return pl.pallas_call(
        body,
        out_shape=out_shape,
        in_specs=[pl.BlockSpec(memory_space=pltpu.SMEM)] + [HBM] * len(far) + [VMEM] * len(near),
        out_specs=[VMEM] * len(out_shape),
        scratch_shapes=scratch,
        compiler_params=pltpu.CompilerParams(vmem_limit_bytes=VMEM_LIMIT),
        cost_estimate=pl.CostEstimate(flops=flops, bytes_accessed=4 << 20, transcendentals=0),
    )(place, *[pltpu.with_memory_space_constraint(a, pltpu.HBM) for a in far], *near)


def local(operator, basis, split_rank):
    place = jnp.stack([lax.axis_index(name) for name in AXES]).astype(jnp.int32)
    f32, bf16 = jnp.float32, jnp.bfloat16
    block = jax.ShapeDtypeStruct((T, T), f32)
    dma = pltpu.SemaphoreType.DMA
    flops = 2 * 3 * 2 * T * T * T * Z

    a = swap(operator)
    right, left = shift_z(basis, 1), shift_z(basis, -1)
    ring = [basis, right, left]
    a = after(a, right, left)
    a2 = flip_yh(a)
    a_near = gather_x(a)
    right, left = shift_z(right, 1), shift_z(left, -1)
    ring += [right, left]
    a_far = gather_x(after(a2, right, left))
    b = swap(after(basis, right, left))
    right, left = shift_z(right, 1), shift_z(left, -1)
    ring += [right, left]
    top, bottom = after((right, left), b)
    by = gather_y(after(b, right, left))
    ring += [shift_z(top[:H], 1), shift_z(bottom[H:], -1)]
    others = [flip_core(r) for r in ring]
    bx = gather_x(after(b, *a_far))

    keep, send = kernel(
        image_kernel, place, a_near + a_far + ring + others, [], [block, block],
        [pltpu.VMEM((22, T, T), f32), pltpu.VMEM((4, H, T), f32), dma((22,)), dma((4,))]
        + [pltpu.VMEM((T, Z * T), bf16)] * 2 + [pltpu.VMEM((2, Z * T, T), bf16)] * 2, flops,
    )
    image = keep + flip_yl(send)
    ix, iy = gather_x(after(image, *bx)), gather_y(after(image, *by))
    four = [jax.ShapeDtypeStruct((4, T, T), bf16)] * 4
    prepared = list(kernel(prepare_kernel, place, bx + by, [], four, [pltpu.VMEM((8, T, T), f32), dma((8,))], flops // 4))
    *out, rh, rl, lh, ll = kernel(first_kernel, place, [], ix + iy + prepared, [block] * (2 * len(FIRST)) + four, flops=flops // 2)
    own, other = dict(zip(FIRST, out)), dict(zip(FIRST, out[len(FIRST):]))
    out = kernel(rest_kernel, place, [], prepared + [rh, rl, lh, ll], [block] * (2 * len(REST)), flops=flops // 2)
    own.update(zip(REST, out))
    other.update(zip(REST, out[len(REST):]))
    part = {}
    for d in FIRST + REST:
        whole = own[d] + flip_core(other[d])
        part[d] = whole[:H], whole[H:]
    right = [part[4][0], part[3][1]]
    left = [part[5][0], part[4][1]]
    right[0], left[1] = shift_z(right[0], 1) + part[3][0], shift_z(left[1], -1) + part[5][1]
    for k in (2, 1, 0):
        right = [shift_z(r, 1) + part[k][h] for h, r in enumerate(right)]
        left = [shift_z(l, -1) + (part[Z - k][h] if k else 0.0) for h, l in enumerate(left)]
    symmetric = 0.5 * flip_pair(jnp.concatenate([right[h] + left[h] for h in range(2)])).T
    row_index = lax.axis_index(ROWS) * T + jnp.arange(T, dtype=jnp.int32)
    col_index = lax.axis_index(COLS) * T + jnp.arange(T, dtype=jnp.int32)
    limit = split_rank[0]
    same = (row_index < limit)[:, None] == (col_index < limit)[None, :]
    return jnp.where(same, symmetric, jnp.float32(0.0))


def solution(mesh):
    fine = Mesh(mesh.devices.reshape(8, 2, 4, 2, 2), AXES)
    in_specs = (P(ROWS, COLS), P(ROWS, COLS), P())
    return jax.shard_map(local, mesh=fine, in_specs=in_specs, out_specs=P(ROWS, COLS), check_vma=False)
```

```python
import jax
import jax.numpy as jnp
from jax import lax
from jax.experimental import pallas as pl
from jax.experimental.pallas import tpu as pltpu
from jax.sharding import Mesh, PartitionSpec as P

Z, X = 8, 4
AXES = ("z", "yl", "x", "yh", "core")
ROWS, COLS = AXES[:2], AXES[2:]
T = 256
H = T // 2
VMEM_LIMIT = 24 * 1024 * 1024
CHUNKS = 2


def _place(d):
    r, c = divmod(d, 16)
    return r // 2, r % 2, c // 4, (c // 2) % 2, c % 2


def _device(z, yl, x, yh, core):
    return (z % Z * 2 + yl) * 16 + (x % X) * 4 + yh * 2 + core


def _send(a, to):
    return lax.ppermute(a, AXES, [(d, _device(*to(*_place(d)))) for d in range(256)])


def swap(a):
    return _send(a, lambda z, yl, x, yh, core: (z, core, x, yh, yl))


def swap_far(a):
    return _send(a, lambda z, yl, x, yh, core: (z, core, x, 1 - yh, yl))


def shift_z(a, k):
    return _send(a, lambda z, yl, x, yh, core: (z + k, yl, x, yh, core))


def shift_x(a, k):
    return _send(a, lambda z, yl, x, yh, core: (z, yl, x + k, yh, core))


def shift_y(a, k):
    def to(z, yl, x, yh, core):
        y = (2 * yh + yl + k) % 4
        return z, y % 2, x, y // 2, core
    return _send(a, to)


def flip_pair(a):
    return _send(a, lambda z, yl, x, yh, core: (z // 2 * 2 + yh, yl, x, z % 2, core))


def flip_yl(a):
    return _send(a, lambda z, yl, x, yh, core: (z, 1 - yl, x, yh, core))


def flip_core(a):
    return _send(a, lambda z, yl, x, yh, core: (z, yl, x, yh, 1 - core))


FOUR = (0, -1, 1, 2)
RING = (0, -1, 1, -2, 2, -3, 3, 4)


def after(a, *others):
    return lax.optimization_barrier((a, others))[0]


def after2(*arrays):
    return lax.optimization_barrier(arrays)


def gather_x(a):
    return [a, shift_x(a, 1), shift_x(a, -1), shift_x(a, 2)]


def gather_y(a):
    return [a, shift_y(a, 1), shift_y(a, -1), shift_y(a, 2)]


def split(a):
    hi = a.astype(jnp.bfloat16)
    return hi, (a - hi.astype(jnp.float32)).astype(jnp.bfloat16)


def panel_place(place, dx, dy):
    return lax.rem(place[2] + dx + X, X) * 2 + lax.rem(place[3] + dy, 2)


def dot3(ah, al, bh, bl):
    def dot(a, b):
        return jnp.dot(a, b, preferred_element_type=jnp.float32)
    return dot(al, bh) + dot(ah, bl) + dot(ah, bh)


def start(pairs, sems):
    copies = []
    for i, (source, destination) in enumerate(pairs):
        if isinstance(source, tuple):
            condition, source, other = source
            pl.when(condition)(pltpu.make_async_copy(source, destination, sems.at[i]).start)
            pl.when(jnp.logical_not(condition))(pltpu.make_async_copy(other, destination, sems.at[i]).start)
            copies.append(pltpu.make_async_copy(source, destination, sems.at[i]))
        else:
            copies.append(pltpu.make_async_copy(source, destination, sems.at[i]))
            copies[-1].start()
    return copies


def ring_pairs(condition, own, other, stage):
    pairs = [((condition, a, b), stage.at[i]) for i, (a, b) in enumerate(zip(own[:7], other[:7]))]
    return pairs + [((condition, own[7 + h], other[7 + h]), stage.at[7, h * H:h * H + H]) for h in range(2)]


def split_ring(z, copies, stage, bh, bl):
    for i, dz in enumerate(RING):
        for copy in copies[i:i + 1] if i < 7 else copies[7:]:
            copy.wait()
        at = pl.multiple_of(lax.rem(z + dz + Z, Z) * T, T)
        bh[pl.ds(at, T)], bl[pl.ds(at, T)] = split(stage[i])


def send_kernel(place, here, right, left, top, bottom, *refs):
    own, other = refs[:9], refs[9:18]
    send, ah, al, stage, sems, b_stage, b_sems, bh, bl = refs[18:]
    z, yl, core = place[0], place[1], place[4]
    near = [r.at[:T] for r in (here, right, left, top)]
    far = [r.at[2 * T:] for r in (here, right, left)] + [bottom.at[H:]]
    copies = start([(r, stage.at[i]) for i, r in enumerate(near + far)], sems)
    b_copies = start(ring_pairs(core != yl, own, other, b_stage), b_sems)
    for i in range(8):
        copies[i].wait()
        at = pl.multiple_of(panel_place(place, FOUR[i % 4], i // 4) * T, T)
        ah[:, pl.ds(at, T)], al[:, pl.ds(at, T)] = split(stage[i])
    split_ring(z, b_copies, b_stage, bh, bl)
    send[...] = dot3(ah[...], al[...], bh[...], bl[...])


def keep_kernel(place, *refs):
    own, other, ah, al = refs[:9], refs[9:18], refs[18], refs[19]
    keep, b_stage, b_sems, bh, bl = refs[20:]
    z, yl, core = place[0], place[1], place[4]
    split_ring(z, start(ring_pairs(core == yl, own, other, b_stage), b_sems), b_stage, bh, bl)
    keep[...] = dot3(ah[...], al[...], bh[...], bl[...])


def prepare_kernel(place, here, right, left, top, bottom, *refs):
    by = refs[:4]
    rh, rl, lh, ll, stage, sems = refs[4:]
    x, y = place[2], 2 * place[3] + place[1]
    pairs = [(r.at[T:2 * T], stage.at[i]) for i, r in enumerate((here, right, left))]
    pairs += [(r, stage.at[4 + i]) for i, r in enumerate(by)]
    pairs += [(top.at[T:], stage.at[3, :H]), (bottom.at[:H], stage.at[3, H:])]
    for copy in start(pairs, sems):
        copy.wait()
    for i, d in enumerate(FOUR):
        at = lax.rem(x + d + 4, 4)
        rh[at], rl[at] = split(stage[i])
        at = lax.rem(y + d + 4, 4)
        lh[at], ll[at] = split(stage[4 + i].T)


FIRST, REST = (4, 3, 5), (2, 6, 1, 7, 0)


def first_kernel(place, *refs):
    ix, iy, basis = refs[:4], refs[4:8], refs[8:12]
    out, image = refs[12:12 + 2 * len(FIRST)], refs[12 + 2 * len(FIRST):]
    rh, rl, lh, ll = image
    x, y = place[2], 2 * place[3] + place[1]
    for ref, d in zip(ix, FOUR):
        at = lax.rem(x + d + 4, 4)
        rh[at], rl[at] = split(ref[...])
    for ref, d in zip(iy, FOUR):
        at = lax.rem(y + d + 4, 4)
        lh[at], ll[at] = split(ref[...].T)
    products(place, basis, image, out, FIRST)


def rest_kernel(place, *refs):
    products(place, refs[:4], refs[4:8], refs[8:], REST)


def products(place, basis, image, out, where):
    brh, brl, blh, bll = basis
    irh, irl, ilh, ill = image
    z, core = place[0], place[4]
    for q, refs in ((1 - core, out[len(where):]), (core, out[:len(where)])):
        for d, ref in zip(where, refs):
            at = lax.rem(z + d, Z)
            r, l = at // 2, 2 * lax.rem(at, 2) + q
            ref[...] = (dot3(ilh[l], ill[l], brh[r], brl[r]) + dot3(blh[l], bll[l], irh[r], irl[r]))


VMEM, HBM = pl.BlockSpec(memory_space=pltpu.VMEM), pl.BlockSpec(memory_space=pltpu.HBM)


def kernel(body, place, far, near, out_shape, scratch=(), flops=0):
    return pl.pallas_call(
        body,
        out_shape=out_shape,
        in_specs=[pl.BlockSpec(memory_space=pltpu.SMEM)] + [HBM] * len(far) + [VMEM] * len(near),
        out_specs=[VMEM] * len(out_shape),
        scratch_shapes=scratch,
        compiler_params=pltpu.CompilerParams(vmem_limit_bytes=VMEM_LIMIT),
        cost_estimate=pl.CostEstimate(flops=flops, bytes_accessed=4 << 20, transcendentals=0),
    )(place, *[pltpu.with_memory_space_constraint(a, pltpu.HBM) for a in far], *near)


def local(operator, basis, split_rank):
    place = jnp.stack([lax.axis_index(name) for name in AXES]).astype(jnp.int32)
    f32, bf16 = jnp.float32, jnp.bfloat16
    block = jax.ShapeDtypeStruct((T, T), f32)
    dma = pltpu.SemaphoreType.DMA
    flops = 2 * 3 * 2 * T * T * T * Z

    right, left = shift_z(basis, 1), shift_z(basis, -1)
    ring = [basis, right, left]
    both = swap(jnp.concatenate([operator, basis]))
    here = after(jnp.concatenate([both, swap_far(operator)]), right, left)
    x_right, x_left = shift_x(here, 1), shift_x(here, -1)
    by = gather_y(after(both[T:], right, left))
    right, left = shift_z(right, 1), shift_z(left, -1)
    ring += [right, left]
    right, left = shift_z(right, 1), shift_z(left, -1)
    ring += [right, left]
    top, bottom = shift_x(after(x_right[:T + H], *by), 1), shift_x(after(x_left[T + H:], *by), -1)
    panel = [here, x_right, x_left, top, bottom]
    ends = [shift_z(right[:H], 1), shift_z(left[H:], -1)]
    others = [flip_core(r) for r in ring] + [flip_core(after(r, top, bottom)) for r in ends]
    ring += ends

    half = jax.ShapeDtypeStruct((T, Z * T), bf16)
    ring_scratch = [pltpu.VMEM((Z, T, T), f32), dma((9,))] + [pltpu.VMEM((Z * T, T), bf16)] * 2
    send, ah, al = kernel(
        send_kernel, place, panel + ring + others, [], [block, half, half],
        [pltpu.VMEM((8, T, T), f32), dma((8,))] + ring_scratch, flops // 2,
    )
    keep, = kernel(keep_kernel, place, ring + others, [ah, al], [block], ring_scratch, flops // 2)
    image = keep + flip_yl(send)
    ix, iy = gather_x(image), gather_y(image)
    four = [jax.ShapeDtypeStruct((4, T, T), bf16)] * 4
    prepared = list(kernel(prepare_kernel, place, panel + by, [], four, [pltpu.VMEM((8, T, T), f32), dma((9,))], flops // 4))
    *out, rh, rl, lh, ll = kernel(first_kernel, place, [], ix + iy + prepared, [block] * (2 * len(FIRST)) + four, flops=flops // 2)
    own, other = dict(zip(FIRST, out)), dict(zip(FIRST, out[len(FIRST):]))
    out = kernel(rest_kernel, place, [], prepared + [rh, rl, lh, ll], [block] * (2 * len(REST)), flops=flops // 2)
    own.update(zip(REST, out))
    other.update(zip(REST, out[len(REST):]))
    part = {}
    for d in FIRST + REST:
        whole = own[d] + flip_core(other[d])
        part[d] = whole[:H], whole[H:]
    right = [part[4][0], part[3][1]]
    left = [part[5][0], part[4][1]]
    right[0], left[1] = shift_z(right[0], 1) + part[3][0], shift_z(left[1], -1) + part[5][1]
    for k in (2, 1, 0):
        right = [shift_z(r, 1) + part[k][h] for h, r in enumerate(right)]
        left = [shift_z(l, -1) + (part[Z - k][h] if k else 0.0) for h, l in enumerate(left)]
    symmetric = 0.5 * flip_pair(jnp.concatenate([right[h] + left[h] for h in range(2)])).T
    row_index = lax.axis_index(ROWS) * T + jnp.arange(T, dtype=jnp.int32)
    col_index = lax.axis_index(COLS) * T + jnp.arange(T, dtype=jnp.int32)
    limit = split_rank[0]
    same = (row_index < limit)[:, None] == (col_index < limit)[None, :]
    return jnp.where(same, symmetric, jnp.float32(0.0))


def solution(mesh):
    fine = Mesh(mesh.devices.reshape(8, 2, 4, 2, 2), AXES)
    in_specs = (P(ROWS, COLS), P(ROWS, COLS), P())
    return jax.shard_map(local, mesh=fine, in_specs=in_specs, out_specs=P(ROWS, COLS), check_vma=False)
```

```python
import jax
import jax.numpy as jnp
from jax import lax
from jax.experimental import pallas as pl
from jax.experimental.pallas import tpu as pltpu
from jax.sharding import Mesh, PartitionSpec as P

Z, X = 8, 4
AXES = ("z", "yl", "x", "yh", "core")
ROWS, COLS = AXES[:2], AXES[2:]
T = 256
H = T // 2
VMEM_LIMIT = 24 * 1024 * 1024
CHUNKS = 2


def _place(d):
    r, c = divmod(d, 16)
    return r // 2, r % 2, c // 4, (c // 2) % 2, c % 2


def _device(z, yl, x, yh, core):
    return (z % Z * 2 + yl) * 16 + (x % X) * 4 + yh * 2 + core


def _send(a, to):
    return lax.ppermute(a, AXES, [(d, _device(*to(*_place(d)))) for d in range(256)])


def swap(a):
    return _send(a, lambda z, yl, x, yh, core: (z, core, x, yh, yl))


def swap_far(a):
    return _send(a, lambda z, yl, x, yh, core: (z, core, x, 1 - yh, yl))


def shift_z(a, k):
    return _send(a, lambda z, yl, x, yh, core: (z + k, yl, x, yh, core))


def shift_x(a, k):
    return _send(a, lambda z, yl, x, yh, core: (z, yl, x + k, yh, core))


def shift_y(a, k):
    def to(z, yl, x, yh, core):
        y = (2 * yh + yl + k) % 4
        return z, y % 2, x, y // 2, core
    return _send(a, to)


def flip_pair(a):
    return _send(a, lambda z, yl, x, yh, core: (z // 2 * 2 + yh, yl, x, z % 2, core))


def flip_yl(a):
    return _send(a, lambda z, yl, x, yh, core: (z, 1 - yl, x, yh, core))


def flip_core(a):
    return _send(a, lambda z, yl, x, yh, core: (z, yl, x, yh, 1 - core))


FOUR = (0, -1, 1, 2)
RING = (0, -1, 1, -2, 2, -3, 3, 4)


def after(a, *others):
    return lax.optimization_barrier((a, others))[0]


def after2(*arrays):
    return lax.optimization_barrier(arrays)


def gather_x(a):
    return [a, shift_x(a, 1), shift_x(a, -1), shift_x(a, 2)]


def gather_y(a):
    return [a, shift_y(a, 1), shift_y(a, -1), shift_y(a, 2)]


def split(a):
    hi = a.astype(jnp.bfloat16)
    return hi, (a - hi.astype(jnp.float32)).astype(jnp.bfloat16)


def panel_place(place, dx, dy):
    return lax.rem(place[2] + dx + X, X) * 2 + lax.rem(place[3] + dy, 2)


def dot3(ah, al, bh, bl):
    def dot(a, b):
        return jnp.dot(a, b, preferred_element_type=jnp.float32)
    return dot(al, bh) + dot(ah, bl) + dot(ah, bh)


def start(pairs, sems):
    copies = []
    for i, (source, destination) in enumerate(pairs):
        if isinstance(source, tuple):
            condition, source, other = source
            pl.when(condition)(pltpu.make_async_copy(source, destination, sems.at[i]).start)
            pl.when(jnp.logical_not(condition))(pltpu.make_async_copy(other, destination, sems.at[i]).start)
            copies.append(pltpu.make_async_copy(source, destination, sems.at[i]))
        else:
            copies.append(pltpu.make_async_copy(source, destination, sems.at[i]))
            copies[-1].start()
    return copies


def ring_pairs(condition, own, other, stage):
    pairs = [((condition, a, b), stage.at[i]) for i, (a, b) in enumerate(zip(own[:7], other[:7]))]
    return pairs + [((condition, own[7 + h], other[7 + h]), stage.at[7, h * H:h * H + H]) for h in range(2)]


def split_ring(z, copies, stage, bh, bl):
    for i, dz in enumerate(RING):
        for copy in copies[i:i + 1] if i < 7 else copies[7:]:
            copy.wait()
        at = pl.multiple_of(lax.rem(z + dz + Z, Z) * T, T)
        bh[pl.ds(at, T)], bl[pl.ds(at, T)] = split(stage[i])


def send_kernel(place, here, right, left, top, bottom, *refs):
    own, other = refs[:9], refs[9:18]
    send, ah, al, stage, sems, b_stage, b_sems, bh, bl = refs[18:]
    z, yl, core = place[0], place[1], place[4]
    near = [r.at[:T] for r in (here, right, left, top)]
    far = [r.at[2 * T:] for r in (here, right, left)] + [bottom.at[H:]]
    copies = start([(r, stage.at[i]) for i, r in enumerate(near + far)], sems)
    b_copies = start(ring_pairs(core != yl, own, other, b_stage), b_sems)
    for i in range(8):
        copies[i].wait()
        at = pl.multiple_of(panel_place(place, FOUR[i % 4], i // 4) * T, T)
        ah[:, pl.ds(at, T)], al[:, pl.ds(at, T)] = split(stage[i])
    split_ring(z, b_copies, b_stage, bh, bl)
    send[...] = dot3(ah[...], al[...], bh[...], bl[...])


def keep_kernel(place, *refs):
    own, other, ah, al = refs[:9], refs[9:18], refs[18], refs[19]
    keep, b_stage, b_sems, bh, bl = refs[20:]
    z, yl, core = place[0], place[1], place[4]
    split_ring(z, start(ring_pairs(core == yl, own, other, b_stage), b_sems), b_stage, bh, bl)
    keep[...] = dot3(ah[...], al[...], bh[...], bl[...])


def prepare_kernel(place, here, right, left, top, bottom, *refs):
    by = refs[:4]
    rh, rl, lh, ll, stage, sems = refs[4:]
    x, y = place[2], 2 * place[3] + place[1]
    pairs = [(r.at[T:2 * T], stage.at[i]) for i, r in enumerate((here, right, left))]
    pairs += [(r, stage.at[4 + i]) for i, r in enumerate(by)]
    pairs += [(top.at[T:], stage.at[3, :H]), (bottom.at[:H], stage.at[3, H:])]
    for copy in start(pairs, sems):
        copy.wait()
    for i, d in enumerate(FOUR):
        at = lax.rem(x + d + 4, 4)
        rh[at], rl[at] = split(stage[i])
        at = lax.rem(y + d + 4, 4)
        lh[at], ll[at] = split(stage[4 + i].T)


FIRST, REST = (4, 3, 5), (2, 6, 1, 7, 0)


def first_kernel(place, *refs):
    ix, iy, basis = refs[:4], refs[4:8], refs[8:12]
    out, image = refs[12:12 + 2 * len(FIRST)], refs[12 + 2 * len(FIRST):]
    rh, rl, lh, ll = image
    x, y = place[2], 2 * place[3] + place[1]
    for ref, d in zip(ix, FOUR):
        at = lax.rem(x + d + 4, 4)
        rh[at], rl[at] = split(ref[...])
    for ref, d in zip(iy, FOUR):
        at = lax.rem(y + d + 4, 4)
        lh[at], ll[at] = split(ref[...].T)
    products(place, basis, image, out, FIRST)


def rest_kernel(place, *refs):
    products(place, refs[:4], refs[4:8], refs[8:], REST)


def products(place, basis, image, out, where):
    brh, brl, blh, bll = basis
    irh, irl, ilh, ill = image
    z, core = place[0], place[4]
    for q, refs in ((1 - core, out[len(where):]), (core, out[:len(where)])):
        for d, ref in zip(where, refs):
            at = lax.rem(z + d, Z)
            r, l = at // 2, 2 * lax.rem(at, 2) + q
            ref[...] = (dot3(ilh[l], ill[l], brh[r], brl[r]) + dot3(blh[l], bll[l], irh[r], irl[r]))


VMEM, HBM = pl.BlockSpec(memory_space=pltpu.VMEM), pl.BlockSpec(memory_space=pltpu.HBM)


def kernel(body, place, far, near, out_shape, scratch=(), flops=0):
    return pl.pallas_call(
        body,
        out_shape=out_shape,
        in_specs=[pl.BlockSpec(memory_space=pltpu.SMEM)] + [HBM] * len(far) + [VMEM] * len(near),
        out_specs=[VMEM] * len(out_shape),
        scratch_shapes=scratch,
        compiler_params=pltpu.CompilerParams(vmem_limit_bytes=VMEM_LIMIT),
        cost_estimate=pl.CostEstimate(flops=flops, bytes_accessed=4 << 20, transcendentals=0),
    )(place, *[pltpu.with_memory_space_constraint(a, pltpu.HBM) for a in far], *near)


def local(operator, basis, split_rank):
    place = jnp.stack([lax.axis_index(name) for name in AXES]).astype(jnp.int32)
    f32, bf16 = jnp.float32, jnp.bfloat16
    block = jax.ShapeDtypeStruct((T, T), f32)
    dma = pltpu.SemaphoreType.DMA
    flops = 2 * 3 * 2 * T * T * T * Z

    right, left = shift_z(basis, 1), shift_z(basis, -1)
    ring = [basis, right, left]
    both = swap(jnp.concatenate([operator, basis]))
    here = after(jnp.concatenate([both, swap_far(operator)]), right, left)
    x_right, x_left = shift_x(here, 1), shift_x(here, -1)
    by = gather_y(after(both[T:], right, left))
    right, left = shift_z(right, 1), shift_z(left, -1)
    ring += [right, left]
    right, left = shift_z(right, 1), shift_z(left, -1)
    ring += [right, left]
    top, bottom = shift_x(after(x_right[:T + H], *by), 1), shift_x(after(x_left[T + H:], *by), -1)
    panel = [here, x_right, x_left, top, bottom]
    ends = [shift_z(right[:H], 1), shift_z(left[H:], -1)]
    others = [flip_core(r) for r in ring] + [flip_core(after(r, top, bottom)) for r in ends]
    ring += ends

    half = jax.ShapeDtypeStruct((T, Z * T), bf16)
    ring_scratch = [pltpu.VMEM((Z, T, T), f32), dma((9,))] + [pltpu.VMEM((Z * T, T), bf16)] * 2
    send, ah, al = kernel(
        send_kernel, place, panel + ring + others, [], [block, half, half],
        [pltpu.VMEM((8, T, T), f32), dma((8,))] + ring_scratch, flops // 2,
    )
    keep, = kernel(keep_kernel, place, ring + others, [ah, al], [block], ring_scratch, flops // 2)
    image = keep + flip_yl(send)
    ix, iy = gather_x(image), gather_y(image)
    four = [jax.ShapeDtypeStruct((4, T, T), bf16)] * 4
    prepared = list(kernel(prepare_kernel, place, panel + by, [], four, [pltpu.VMEM((8, T, T), f32), dma((9,))], flops // 4))
    *out, rh, rl, lh, ll = kernel(first_kernel, place, [], ix + iy + prepared, [block] * (2 * len(FIRST)) + four, flops=flops // 2)
    own, other = dict(zip(FIRST, out)), dict(zip(FIRST, out[len(FIRST):]))
    out = kernel(rest_kernel, place, [], prepared + [rh, rl, lh, ll], [block] * (2 * len(REST)), flops=flops // 2)
    own.update(zip(REST, out))
    other.update(zip(REST, out[len(REST):]))
    part = {d: own[d] + flip_core(other[d]) for d in FIRST + REST}
    right, left = part[3], part[4]
    for k in range(1, 4):
        right, left = shift_z(right, 1) + part[3 - k], shift_z(left, -1) + part[4 + k]
    symmetric = 0.5 * flip_pair(right + shift_z(left, -1)).T
    row_index = lax.axis_index(ROWS) * T + jnp.arange(T, dtype=jnp.int32)
    col_index = lax.axis_index(COLS) * T + jnp.arange(T, dtype=jnp.int32)
    limit = split_rank[0]
    same = (row_index < limit)[:, None] == (col_index < limit)[None, :]
    return jnp.where(same, symmetric, jnp.float32(0.0))


def solution(mesh):
    fine = Mesh(mesh.devices.reshape(8, 2, 4, 2, 2), AXES)
    in_specs = (P(ROWS, COLS), P(ROWS, COLS), P())
    return jax.shard_map(local, mesh=fine, in_specs=in_specs, out_specs=P(ROWS, COLS), check_vma=False)
```

```python
import jax
import jax.numpy as jnp
from jax import lax
from jax.experimental import pallas as pl
from jax.experimental.pallas import tpu as pltpu
from jax.sharding import Mesh, PartitionSpec as P

Z, X = 8, 4
AXES = ("z", "yl", "x", "yh", "core")
ROWS, COLS = AXES[:2], AXES[2:]
T = 256
H = T // 2
VMEM_LIMIT = 24 * 1024 * 1024
CHUNKS = 2


def _place(d):
    r, c = divmod(d, 16)
    return r // 2, r % 2, c // 4, (c // 2) % 2, c % 2


def _device(z, yl, x, yh, core):
    return (z % Z * 2 + yl) * 16 + (x % X) * 4 + yh * 2 + core


def _send(a, to):
    return lax.ppermute(a, AXES, [(d, _device(*to(*_place(d)))) for d in range(256)])


def swap(a):
    return _send(a, lambda z, yl, x, yh, core: (z, core, x, yh, yl))


def swap_far(a):
    return _send(a, lambda z, yl, x, yh, core: (z, core, x, 1 - yh, yl))


def shift_z(a, k):
    return _send(a, lambda z, yl, x, yh, core: (z + k, yl, x, yh, core))


def shift_x(a, k):
    return _send(a, lambda z, yl, x, yh, core: (z, yl, x + k, yh, core))


def shift_y(a, k):
    def to(z, yl, x, yh, core):
        y = (2 * yh + yl + k) % 4
        return z, y % 2, x, y // 2, core
    return _send(a, to)


def flip_pair(a):
    return _send(a, lambda z, yl, x, yh, core: (z // 2 * 2 + yh, yl, x, z % 2, core))


def flip_yl(a):
    return _send(a, lambda z, yl, x, yh, core: (z, 1 - yl, x, yh, core))


def flip_core(a):
    return _send(a, lambda z, yl, x, yh, core: (z, yl, x, yh, 1 - core))


FOUR = (0, -1, 1, 2)
RING = (0, -1, 1, -2, 2, -3, 3, 4)


def after(a, *others):
    return lax.optimization_barrier((a, others))[0]


def after2(*arrays):
    return lax.optimization_barrier(arrays)


def gather_x(a):
    return [a, shift_x(a, 1), shift_x(a, -1), shift_x(a, 2)]


def gather_y(a):
    return [a, shift_y(a, 1), shift_y(a, -1), shift_y(a, 2)]


def split(a):
    hi = a.astype(jnp.bfloat16)
    return hi, (a - hi.astype(jnp.float32)).astype(jnp.bfloat16)


def panel_place(place, dx, dy):
    return lax.rem(place[2] + dx + X, X) * 2 + lax.rem(place[3] + dy, 2)


def dot3(ah, al, bh, bl):
    def dot(a, b):
        return jnp.dot(a, b, preferred_element_type=jnp.float32)
    return dot(al, bh) + dot(ah, bl) + dot(ah, bh)


def start(pairs, sems):
    copies = []
    for i, (source, destination) in enumerate(pairs):
        if isinstance(source, tuple):
            condition, source, other = source
            pl.when(condition)(pltpu.make_async_copy(source, destination, sems.at[i]).start)
            pl.when(jnp.logical_not(condition))(pltpu.make_async_copy(other, destination, sems.at[i]).start)
            copies.append(pltpu.make_async_copy(source, destination, sems.at[i]))
        else:
            copies.append(pltpu.make_async_copy(source, destination, sems.at[i]))
            copies[-1].start()
    return copies


def ring_pairs(condition, own, other, stage):
    pairs = [((condition, a, b), stage.at[i]) for i, (a, b) in enumerate(zip(own[:7], other[:7]))]
    return pairs + [((condition, own[7 + h], other[7 + h]), stage.at[7, h * H:h * H + H]) for h in range(2)]


def split_ring(z, copies, stage, bh, bl):
    for i, dz in enumerate(RING):
        for copy in copies[i:i + 1] if i < 7 else copies[7:]:
            copy.wait()
        at = pl.multiple_of(lax.rem(z + dz + Z, Z) * T, T)
        bh[pl.ds(at, T)], bl[pl.ds(at, T)] = split(stage[i])


def send_kernel(place, here, right, left, top, bottom, *refs):
    own, other = refs[:9], refs[9:18]
    send, ah, al, stage, sems, b_stage, b_sems, bh, bl = refs[18:]
    z, yl, core = place[0], place[1], place[4]
    near = [r.at[:T] for r in (here, right, left, top)]
    far = [r.at[2 * T:] for r in (here, right, left)] + [bottom.at[H:]]
    copies = start([(r, stage.at[i]) for i, r in enumerate(near + far)], sems)
    b_copies = start(ring_pairs(core != yl, own, other, b_stage), b_sems)
    for i in range(8):
        copies[i].wait()
        at = pl.multiple_of(panel_place(place, FOUR[i % 4], i // 4) * T, T)
        ah[:, pl.ds(at, T)], al[:, pl.ds(at, T)] = split(stage[i])
    split_ring(z, b_copies, b_stage, bh, bl)
    send[...] = dot3(ah[...], al[...], bh[...], bl[...])


def keep_kernel(place, *refs):
    own, other, ah, al = refs[:9], refs[9:18], refs[18], refs[19]
    keep, b_stage, b_sems, bh, bl = refs[20:]
    z, yl, core = place[0], place[1], place[4]
    split_ring(z, start(ring_pairs(core == yl, own, other, b_stage), b_sems), b_stage, bh, bl)
    keep[...] = dot3(ah[...], al[...], bh[...], bl[...])


def prepare_kernel(place, here, right, left, top, bottom, *refs):
    by = refs[:4]
    rh, rl, lh, ll, stage, sems = refs[4:]
    x, y = place[2], 2 * place[3] + place[1]
    pairs = [(r.at[T:2 * T], stage.at[i]) for i, r in enumerate((here, right, left))]
    pairs += [(r, stage.at[4 + i]) for i, r in enumerate(by)]
    pairs += [(top.at[T:], stage.at[3, :H]), (bottom.at[:H], stage.at[3, H:])]
    for copy in start(pairs, sems):
        copy.wait()
    for i, d in enumerate(FOUR):
        at = lax.rem(x + d + 4, 4)
        rh[at], rl[at] = split(stage[i])
        at = lax.rem(y + d + 4, 4)
        lh[at], ll[at] = split(stage[4 + i].T)


FIRST, REST = (4, 3, 5), (2, 6, 1, 7, 0)


def first_kernel(place, *refs):
    ix, iy, basis = refs[:4], refs[4:8], refs[8:12]
    out, image = refs[12:12 + 2 * len(FIRST)], refs[12 + 2 * len(FIRST):]
    rh, rl, lh, ll = image
    x, y = place[2], 2 * place[3] + place[1]
    for ref, d in zip(ix, FOUR):
        at = lax.rem(x + d + 4, 4)
        rh[at], rl[at] = split(ref[...])
    for ref, d in zip(iy, FOUR):
        at = lax.rem(y + d + 4, 4)
        lh[at], ll[at] = split(ref[...].T)
    products(place, basis, image, out, FIRST)


def rest_kernel(place, *refs):
    products(place, refs[:4], refs[4:8], refs[8:], REST)


def products(place, basis, image, out, where):
    brh, brl, blh, bll = basis
    irh, irl, ilh, ill = image
    z, core = place[0], place[4]
    for q, refs in ((1 - core, out[len(where):]), (core, out[:len(where)])):
        for d, ref in zip(where, refs):
            at = lax.rem(z + d, Z)
            r, l = at // 2, 2 * lax.rem(at, 2) + q
            ref[...] = (dot3(ilh[l], ill[l], brh[r], brl[r]) + dot3(blh[l], bll[l], irh[r], irl[r]))


VMEM, HBM = pl.BlockSpec(memory_space=pltpu.VMEM), pl.BlockSpec(memory_space=pltpu.HBM)


def kernel(body, place, far, near, out_shape, scratch=(), flops=0):
    return pl.pallas_call(
        body,
        out_shape=out_shape,
        in_specs=[pl.BlockSpec(memory_space=pltpu.SMEM)] + [HBM] * len(far) + [VMEM] * len(near),
        out_specs=[VMEM] * len(out_shape),
        scratch_shapes=scratch,
        compiler_params=pltpu.CompilerParams(vmem_limit_bytes=VMEM_LIMIT),
        cost_estimate=pl.CostEstimate(flops=flops, bytes_accessed=4 << 20, transcendentals=0),
    )(place, *[pltpu.with_memory_space_constraint(a, pltpu.HBM) for a in far], *near)


def local(operator, basis, split_rank):
    place = jnp.stack([lax.axis_index(name) for name in AXES]).astype(jnp.int32)
    f32, bf16 = jnp.float32, jnp.bfloat16
    block = jax.ShapeDtypeStruct((T, T), f32)
    dma = pltpu.SemaphoreType.DMA
    flops = 2 * 3 * 2 * T * T * T * Z

    right, left = shift_z(basis, 1), shift_z(basis, -1)
    ring = [basis, right, left]
    both = swap(jnp.concatenate([operator, basis]))
    here = after(jnp.concatenate([both, swap_far(operator)]), right, left)
    x_right, x_left = shift_x(here, 1), shift_x(here, -1)
    by = gather_y(after(both[T:], right, left))
    right, left = shift_z(right, 1), shift_z(left, -1)
    ring += [right, left]
    right, left = shift_z(right, 1), shift_z(left, -1)
    ring += [right, left]
    top, bottom = shift_x(x_right[:T + H], 1), shift_x(x_left[T + H:], -1)
    panel = [here, x_right, x_left, top, bottom]
    ends = [shift_z(right[:H], 1), shift_z(left[H:], -1)]
    others = [flip_core(r) for r in ring] + [flip_core(r) for r in ends]
    ring += ends

    half = jax.ShapeDtypeStruct((T, Z * T), bf16)
    ring_scratch = [pltpu.VMEM((Z, T, T), f32), dma((9,))] + [pltpu.VMEM((Z * T, T), bf16)] * 2
    send, ah, al = kernel(
        send_kernel, place, panel + ring + others, [], [block, half, half],
        [pltpu.VMEM((8, T, T), f32), dma((8,))] + ring_scratch, flops // 2,
    )
    keep, = kernel(keep_kernel, place, ring + others, [ah, al], [block], ring_scratch, flops // 2)
    image = keep + flip_yl(send)
    ix, iy = gather_x(image), gather_y(after(image, *by))
    four = [jax.ShapeDtypeStruct((4, T, T), bf16)] * 4
    prepared = list(kernel(prepare_kernel, place, panel + by, [], four, [pltpu.VMEM((8, T, T), f32), dma((9,))], flops // 4))
    *out, rh, rl, lh, ll = kernel(first_kernel, place, [], ix + iy + prepared, [block] * (2 * len(FIRST)) + four, flops=flops // 2)
    own, other = dict(zip(FIRST, out)), dict(zip(FIRST, out[len(FIRST):]))
    out = kernel(rest_kernel, place, [], prepared + [rh, rl, lh, ll], [block] * (2 * len(REST)), flops=flops // 2)
    own.update(zip(REST, out))
    other.update(zip(REST, out[len(REST):]))
    part = {d: own[d] + flip_core(other[d]) for d in FIRST + REST}
    right, left = part[3], part[4]
    for k in range(1, 4):
        right, left = shift_z(right, 1) + part[3 - k], shift_z(left, -1) + part[4 + k]
    symmetric = 0.5 * flip_pair(right + shift_z(left, -1)).T
    row_index = lax.axis_index(ROWS) * T + jnp.arange(T, dtype=jnp.int32)
    col_index = lax.axis_index(COLS) * T + jnp.arange(T, dtype=jnp.int32)
    limit = split_rank[0]
    same = (row_index < limit)[:, None] == (col_index < limit)[None, :]
    return jnp.where(same, symmetric, jnp.float32(0.0))


def solution(mesh):
    fine = Mesh(mesh.devices.reshape(8, 2, 4, 2, 2), AXES)
    in_specs = (P(ROWS, COLS), P(ROWS, COLS), P())
    return jax.shard_map(local, mesh=fine, in_specs=in_specs, out_specs=P(ROWS, COLS), check_vma=False)
```

```python
import jax
import jax.numpy as jnp
from jax import lax
from jax.experimental import pallas as pl
from jax.experimental.pallas import tpu as pltpu
from jax.sharding import Mesh, PartitionSpec as P

Z, X = 8, 4
AXES = ("z", "yl", "x", "yh", "core")
ROWS, COLS = AXES[:2], AXES[2:]
T = 256
H = T // 2
VMEM_LIMIT = 24 * 1024 * 1024
CHUNKS = 2


def _place(d):
    r, c = divmod(d, 16)
    return r // 2, r % 2, c // 4, (c // 2) % 2, c % 2


def _device(z, yl, x, yh, core):
    return (z % Z * 2 + yl) * 16 + (x % X) * 4 + yh * 2 + core


def _send(a, to):
    return lax.ppermute(a, AXES, [(d, _device(*to(*_place(d)))) for d in range(256)])


def swap(a):
    return _send(a, lambda z, yl, x, yh, core: (z, core, x, yh, yl))


def swap_far(a):
    return _send(a, lambda z, yl, x, yh, core: (z, core, x, 1 - yh, yl))


def shift_z(a, k):
    return _send(a, lambda z, yl, x, yh, core: (z + k, yl, x, yh, core))


def shift_x(a, k):
    return _send(a, lambda z, yl, x, yh, core: (z, yl, x + k, yh, core))


def shift_y(a, k):
    def to(z, yl, x, yh, core):
        y = (2 * yh + yl + k) % 4
        return z, y % 2, x, y // 2, core
    return _send(a, to)


def flip_pair(a):
    return _send(a, lambda z, yl, x, yh, core: (z // 2 * 2 + yh, yl, x, z % 2, core))


def flip_yl(a):
    return _send(a, lambda z, yl, x, yh, core: (z, 1 - yl, x, yh, core))


def flip_core(a):
    return _send(a, lambda z, yl, x, yh, core: (z, yl, x, yh, 1 - core))


FOUR = (0, -1, 1, 2)
RING = (0, -1, 1, -2, 2, -3, 3, 4)


def after(a, *others):
    return lax.optimization_barrier((a, others))[0]


def after2(*arrays):
    return lax.optimization_barrier(arrays)


def gather_x(a):
    return [a, shift_x(a, 1), shift_x(a, -1), shift_x(a, 2)]


def gather_y(a):
    return [a, shift_y(a, 1), shift_y(a, -1), shift_y(a, 2)]


def split(a):
    hi = a.astype(jnp.bfloat16)
    return hi, (a - hi.astype(jnp.float32)).astype(jnp.bfloat16)


def panel_place(place, dx, dy):
    return lax.rem(place[2] + dx + X, X) * 2 + lax.rem(place[3] + dy, 2)


def dot3(ah, al, bh, bl):
    def dot(a, b):
        return jnp.dot(a, b, preferred_element_type=jnp.float32)
    return dot(al, bh) + dot(ah, bl) + dot(ah, bh)


def start(pairs, sems):
    copies = []
    for i, (source, destination) in enumerate(pairs):
        if isinstance(source, tuple):
            condition, source, other = source
            pl.when(condition)(pltpu.make_async_copy(source, destination, sems.at[i]).start)
            pl.when(jnp.logical_not(condition))(pltpu.make_async_copy(other, destination, sems.at[i]).start)
            copies.append(pltpu.make_async_copy(source, destination, sems.at[i]))
        else:
            copies.append(pltpu.make_async_copy(source, destination, sems.at[i]))
            copies[-1].start()
    return copies


def ring_pairs(condition, own, other, stage):
    pairs = [((condition, a, b), stage.at[i]) for i, (a, b) in enumerate(zip(own[:7], other[:7]))]
    return pairs + [((condition, own[7 + h], other[7 + h]), stage.at[7, h * H:h * H + H]) for h in range(2)]


def split_ring(z, copies, stage, bh, bl):
    for i, dz in enumerate(RING):
        for copy in copies[i:i + 1] if i < 7 else copies[7:]:
            copy.wait()
        at = pl.multiple_of(lax.rem(z + dz + Z, Z) * T, T)
        bh[pl.ds(at, T)], bl[pl.ds(at, T)] = split(stage[i])


def send_kernel(place, here, right, left, top, bottom, *refs):
    own, other = refs[:9], refs[9:18]
    send, ah, al, stage, sems, b_stage, b_sems, bh, bl = refs[18:]
    z, yl, core = place[0], place[1], place[4]
    near = [r.at[:T] for r in (here, right, left, top)]
    far = [r.at[2 * T:] for r in (here, right, left)] + [bottom.at[H:]]
    copies = start([(r, stage.at[i]) for i, r in enumerate(near + far)], sems)
    b_copies = start(ring_pairs(core != yl, own, other, b_stage), b_sems)
    for i in range(8):
        copies[i].wait()
        at = pl.multiple_of(panel_place(place, FOUR[i % 4], i // 4) * T, T)
        ah[:, pl.ds(at, T)], al[:, pl.ds(at, T)] = split(stage[i])
    split_ring(z, b_copies, b_stage, bh, bl)
    send[...] = dot3(ah[...], al[...], bh[...], bl[...])


def keep_kernel(place, *refs):
    own, other, ah, al = refs[:9], refs[9:18], refs[18], refs[19]
    keep, b_stage, b_sems, bh, bl = refs[20:]
    z, yl, core = place[0], place[1], place[4]
    split_ring(z, start(ring_pairs(core == yl, own, other, b_stage), b_sems), b_stage, bh, bl)
    keep[...] = dot3(ah[...], al[...], bh[...], bl[...])


def prepare_kernel(place, here, right, left, top, bottom, *refs):
    by = refs[:4]
    rh, rl, lh, ll, stage, sems = refs[4:]
    x, y = place[2], 2 * place[3] + place[1]
    pairs = [(r.at[T:2 * T], stage.at[i]) for i, r in enumerate((here, right, left))]
    pairs += [(r, stage.at[4 + i]) for i, r in enumerate(by)]
    pairs += [(top.at[T:], stage.at[3, :H]), (bottom.at[:H], stage.at[3, H:])]
    for copy in start(pairs, sems):
        copy.wait()
    for i, d in enumerate(FOUR):
        at = lax.rem(x + d + 4, 4)
        rh[at], rl[at] = split(stage[i])
        at = lax.rem(y + d + 4, 4)
        lh[at], ll[at] = split(stage[4 + i].T)


FIRST, REST = (4, 3, 5), (2, 6, 1, 7, 0)


def first_kernel(place, *refs):
    ix, iy, basis = refs[:4], refs[4:8], refs[8:12]
    out, image = refs[12:12 + 2 * len(FIRST)], refs[12 + 2 * len(FIRST):]
    rh, rl, lh, ll = image
    x, y = place[2], 2 * place[3] + place[1]
    for ref, d in zip(ix, FOUR):
        at = lax.rem(x + d + 4, 4)
        rh[at], rl[at] = split(ref[...])
    for ref, d in zip(iy, FOUR):
        at = lax.rem(y + d + 4, 4)
        lh[at], ll[at] = split(ref[...].T)
    products(place, basis, image, out, FIRST)


def rest_kernel(place, *refs):
    products(place, refs[:4], refs[4:8], refs[8:], REST)


def products(place, basis, image, out, where):
    brh, brl, blh, bll = basis
    irh, irl, ilh, ill = image
    z, core = place[0], place[4]
    for q, refs in ((1 - core, out[len(where):]), (core, out[:len(where)])):
        for d, ref in zip(where, refs):
            at = lax.rem(z + d, Z)
            r, l = at // 2, 2 * lax.rem(at, 2) + q
            ref[...] = (dot3(ilh[l], ill[l], brh[r], brl[r]) + dot3(blh[l], bll[l], irh[r], irl[r]))


VMEM, HBM = pl.BlockSpec(memory_space=pltpu.VMEM), pl.BlockSpec(memory_space=pltpu.HBM)


def kernel(body, place, far, near, out_shape, scratch=(), flops=0):
    return pl.pallas_call(
        body,
        out_shape=out_shape,
        in_specs=[pl.BlockSpec(memory_space=pltpu.SMEM)] + [HBM] * len(far) + [VMEM] * len(near),
        out_specs=[VMEM] * len(out_shape),
        scratch_shapes=scratch,
        compiler_params=pltpu.CompilerParams(vmem_limit_bytes=VMEM_LIMIT),
        cost_estimate=pl.CostEstimate(flops=flops, bytes_accessed=4 << 20, transcendentals=0),
    )(place, *[pltpu.with_memory_space_constraint(a, pltpu.HBM) for a in far], *near)


def local(operator, basis, split_rank):
    place = jnp.stack([lax.axis_index(name) for name in AXES]).astype(jnp.int32)
    f32, bf16 = jnp.float32, jnp.bfloat16
    block = jax.ShapeDtypeStruct((T, T), f32)
    dma = pltpu.SemaphoreType.DMA
    flops = 2 * 3 * 2 * T * T * T * Z

    right, left = shift_z(basis, 1), shift_z(basis, -1)
    ring = [basis, right, left]
    both = swap(jnp.concatenate([operator, basis]))
    here = after(jnp.concatenate([both, swap_far(operator)]), right, left)
    x_right, x_left = shift_x(here, 1), shift_x(here, -1)
    by = gather_y(after(both[T:], right, left))
    right, left = shift_z(right, 1), shift_z(left, -1)
    ring += [right, left]
    right, left = shift_z(after(right, left), 1), shift_z(after(left, right), -1)
    ring += [right, left]
    top, bottom = shift_x(after(x_right[:T + H], *by), 1), shift_x(after(x_left[T + H:], *by), -1)
    panel = [here, x_right, x_left, top, bottom]
    ends = [shift_z(right[:H], 1), shift_z(left[H:], -1)]
    others = [flip_core(r) for r in ring] + [flip_core(after(r, top, bottom)) for r in ends]
    ring += ends

    half = jax.ShapeDtypeStruct((T, Z * T), bf16)
    ring_scratch = [pltpu.VMEM((Z, T, T), f32), dma((9,))] + [pltpu.VMEM((Z * T, T), bf16)] * 2
    send, ah, al = kernel(
        send_kernel, place, panel + ring + others, [], [block, half, half],
        [pltpu.VMEM((8, T, T), f32), dma((8,))] + ring_scratch, flops // 2,
    )
    keep, = kernel(keep_kernel, place, ring + others, [ah, al], [block], ring_scratch, flops // 2)
    image = keep + flip_yl(send)
    ix, iy = gather_x(image), gather_y(image)
    four = [jax.ShapeDtypeStruct((4, T, T), bf16)] * 4
    prepared = list(kernel(prepare_kernel, place, panel + by, [], four, [pltpu.VMEM((8, T, T), f32), dma((9,))], flops // 4))
    *out, rh, rl, lh, ll = kernel(first_kernel, place, [], ix + iy + prepared, [block] * (2 * len(FIRST)) + four, flops=flops // 2)
    own, other = dict(zip(FIRST, out)), dict(zip(FIRST, out[len(FIRST):]))
    out = kernel(rest_kernel, place, [], prepared + [rh, rl, lh, ll], [block] * (2 * len(REST)), flops=flops // 2)
    own.update(zip(REST, out))
    other.update(zip(REST, out[len(REST):]))
    part = {d: own[d] + flip_core(other[d]) for d in FIRST + REST}
    right, left = part[3], part[4]
    for k in range(1, 4):
        right, left = shift_z(right, 1) + part[3 - k], shift_z(left, -1) + part[4 + k]
    symmetric = 0.5 * flip_pair(right + shift_z(left, -1)).T
    row_index = lax.axis_index(ROWS) * T + jnp.arange(T, dtype=jnp.int32)
    col_index = lax.axis_index(COLS) * T + jnp.arange(T, dtype=jnp.int32)
    limit = split_rank[0]
    same = (row_index < limit)[:, None] == (col_index < limit)[None, :]
    return jnp.where(same, symmetric, jnp.float32(0.0))


def solution(mesh):
    fine = Mesh(mesh.devices.reshape(8, 2, 4, 2, 2), AXES)
    in_specs = (P(ROWS, COLS), P(ROWS, COLS), P())
    return jax.shard_map(local, mesh=fine, in_specs=in_specs, out_specs=P(ROWS, COLS), check_vma=False)
```
